512 devices in a mesh: dp: 64 (over y, z), head: 8 (over x, core).
Axes of the slice: x: 4, y: 8, z: 8, core: 2. Of those that a mesh axis runs over, the one named last changes fastest.
Arguments:
- queries: bfloat16 [65536, 4096], P(('dp', 'head')), may hold values from -6 to 6
- key_rows: bfloat16 [65536, 1024], P(('dp', 'head')), may hold values from -6 to 6
- values: bfloat16 [65536, 1024], P(('dp', 'head')), may hold values from -6 to 6
- cotangent: bfloat16 [65536, 4096], P(('dp', 'head')), may hold values from -6 to 6
- block_route: int32 [512, 2], replicated, may hold values from 0 to 63, as said below
- doc_start: int32 [512], replicated, may hold values from 0 to 65408, as said below
Outputs:
- grad_queries: bfloat16 [65536, 4096], P('dp', 'head')
- grad_keys: bfloat16 [65536, 1024], P('dp', 'head')
- grad_values: bfloat16 [65536, 1024], P('dp', 'head')
The draws below stay inside these ranges and needn't reach their ends.
Inputs may be any that keep to these rules, and one draw needn't show every extreme that they name: `block_route`: row b gives the dp index and the slot, among that index's 8 slots, of block b in the attention placement. The dp indices 2p and 2p + 1 are partners: each hands exactly half of its aligned bins of 4 blocks, whole, to the other, into the slots of the bins that the other hands over, in order; every other block keeps its dp index and slot. After the move no dp index holds more than 16 pairs of a query block and a key block at or before it in the same document. `doc_start`: each entry is the first token of its block's document; documents are runs of whole blocks inside aligned bins of 4 blocks.
All inputs are finite; a program needn't handle non-finite values.
Results may differ from the reference program's by a relative error of at most 0.023.
Values may be sent and summed in bfloat16 or wider, within the bound.
A program may use at most 64 MiB of HBM per device.

```python
import jax
import jax.numpy as jnp
import numpy as np
from jax import lax

HEADS = 32
KV_HEADS = 8
HEAD_DIM = 128
BLOCK = 128
BPD = 8
BLOCKS = 512
TOKENS = 65536
N_DP = 64


HEAVY_BINS = np.array([[1, 0, 0, 0], [1, 0, 0, 1], [1, 1, 0, 0]], dtype=np.int32)


LIGHT_BINS = np.array([[1, 0, 1, 0], [1, 0, 1, 1], [1, 1, 0, 1], [1, 1, 1, 0], [1, 1, 1, 1]], dtype=np.int32)


def bin_order(sub_key):
    return jax.random.permutation(sub_key, BPD // 4)


def plan_tables(key):
    bin_count = BPD // 4
    pairs = N_DP // 2
    key_side, key_heavy, key_light, key_send = jax.random.split(key, 4)
    heavy_side = jax.random.randint(key_side, (pairs,), 0, 2)
    heavy_kind = jax.random.randint(key_heavy, (pairs, bin_count), 0, 3)
    light_kind = jax.random.randint(key_light, (pairs, bin_count), 0, 5)
    pair_index = jnp.arange(pairs)
    heavy_kind = jnp.where(pair_index[:, None] == 0, 0, heavy_kind)
    light_kind = jnp.where(pair_index[:, None] == 0, 0, light_kind)
    light_kind = jnp.where(pair_index[:, None] == pairs - 1, 4, light_kind)
    heavy_side = jnp.where(pair_index == pairs - 1, 0, heavy_side)
    heavy_flags = jnp.asarray(HEAVY_BINS)[heavy_kind]
    light_flags = jnp.asarray(LIGHT_BINS)[light_kind]
    side_flag = heavy_side[:, None, None]
    even_flags = jnp.where(side_flag == 0, heavy_flags, light_flags)
    odd_flags = jnp.where(side_flag == 0, light_flags, heavy_flags)
    flags = jnp.stack([even_flags, odd_flags], axis=1).reshape(N_DP, bin_count, 4)
    within = jnp.arange(4, dtype=jnp.int32)
    marked = jnp.where(flags == 1, within, 0)
    first_mark = lax.cummax(marked, axis=2)
    block_ids = jnp.arange(N_DP * BPD, dtype=jnp.int32).reshape(N_DP, bin_count, 4)
    doc_first = (block_ids - within + first_mark) * BLOCK
    bin_ranks = jax.vmap(bin_order)(jax.random.split(key_send, N_DP))
    sent_bins = bin_ranks < bin_count // 2
    moved_out = jnp.broadcast_to(sent_bins[:, :, None], (N_DP, bin_count, 4)).reshape(N_DP, BPD)
    slot_index = jnp.arange(BPD, dtype=jnp.int32)
    vacated = jnp.argsort(jnp.where(moved_out, 0, 1), axis=1, stable=True)[:, :BPD // 2]
    move_rank = jnp.clip(jnp.cumsum(moved_out.astype(jnp.int32), axis=1) - 1, 0, BPD // 2 - 1)
    partner = jnp.arange(N_DP, dtype=jnp.int32) ^ 1
    target_slot = jnp.take_along_axis(vacated[partner], move_rank, axis=1)
    dest_slot = jnp.where(moved_out, target_slot, slot_index[None, :])
    dest_dp = jnp.where(moved_out, partner[:, None], jnp.arange(N_DP, dtype=jnp.int32)[:, None])
    route = jnp.stack([dest_dp, dest_slot], axis=-1).reshape(N_DP * BPD, 2)
    return (doc_first.reshape(N_DP * BPD).astype(jnp.int32), route.astype(jnp.int32))


def draw_block_route(key, part):
    return plan_tables(jax.random.fold_in(key, 3))[1]


def draw_doc_start(key, part):
    return plan_tables(jax.random.fold_in(key, 3))[0]


def draw_queries(key, part):
    shape = (TOKENS, HEADS * HEAD_DIM)
    result = jnp.clip(jax.random.normal(jax.random.fold_in(key, 11), shape, jnp.float32), -6.0, 6.0)
    return result.astype(jnp.bfloat16)


def draw_key_rows(key, part):
    shape = (TOKENS, KV_HEADS * HEAD_DIM)
    result = jnp.clip(jax.random.normal(jax.random.fold_in(key, 13), shape, jnp.float32), -6.0, 6.0)
    return result.astype(jnp.bfloat16)


def shard_levels(key, shape, cuts, low, largest):
    factor_of, own = 1.0, jax.random.fold_in(key, 6)
    for dim, blocks in cuts:
        steps = jnp.exp(jax.random.uniform(jax.random.fold_in(own, dim), (blocks,), jnp.float32, low / len(cuts), largest / len(cuts)))
        factor_of = factor_of * jnp.repeat(steps, shape[dim] // blocks).reshape([-1 if axis == dim else 1 for axis in range(len(shape))])
    return factor_of


def centred(rng, extent, width, limit, cuts=(), held_as=jnp.bfloat16):
    entries = jax.random.normal(rng, extent, jnp.float32) * width
    if len(cuts) > 0:
        entries = shard_levels(rng, extent, cuts, -0.22, 0.18) * entries
    return jnp.clip(entries, min=-limit, max=limit).astype(held_as)


def setup_inputs(seed: int = 0) -> dict:
    arg_keys = jax.random.split(jax.random.key(seed), 7)
    return {
        "queries": draw_queries(jax.random.fold_in(arg_keys[6], 71), 0),
        "key_rows": draw_key_rows(jax.random.fold_in(arg_keys[6], 71), 0),
        "values": centred(arg_keys[2], (TOKENS, KV_HEADS * HEAD_DIM), 1.0, 6.0, ((0, 512),)),
        "cotangent": centred(arg_keys[3], (TOKENS, HEADS * HEAD_DIM), 1.0, 6.0, ((0, 512),)),
        "block_route": draw_block_route(jax.random.fold_in(arg_keys[6], 71), 0),
        "doc_start": draw_doc_start(jax.random.fold_in(arg_keys[6], 71), 0),
    }


def bin_grads(queries, key_rows, values, cotangent, token_doc, bin_index):
    bin_span = 4 * BLOCK
    per_group = HEADS // KV_HEADS
    softmax_scale = HEAD_DIM ** -0.5
    row_start = (bin_index * bin_span).astype(jnp.int32)

    def rows_of(tensor):
        return lax.dynamic_slice_in_dim(tensor, row_start, bin_span, 0)

    q_bin = rows_of(queries).astype(jnp.float32).reshape(bin_span, KV_HEADS, per_group, HEAD_DIM)
    k_bin = rows_of(key_rows).astype(jnp.float32).reshape(bin_span, KV_HEADS, HEAD_DIM)
    v_bin = rows_of(values).astype(jnp.float32).reshape(bin_span, KV_HEADS, HEAD_DIM)
    d_bin = rows_of(cotangent).astype(jnp.float32).reshape(bin_span, KV_HEADS, per_group, HEAD_DIM)
    doc_bin = rows_of(token_doc)
    position = jnp.arange(bin_span, dtype=jnp.int32)
    allowed = (doc_bin[:, None] == doc_bin[None, :]) & (position[None, :] <= position[:, None])
    scores = jnp.einsum("qcgd,kcd->cgqk", q_bin, k_bin) * softmax_scale
    masked = jnp.where(allowed, scores, -jnp.inf)
    top_score = jnp.max(masked, axis=-1, keepdims=True)
    exp_scores = jnp.exp(masked - top_score)
    total = jnp.sum(exp_scores, axis=-1, keepdims=True)
    weights = lax.optimization_barrier((exp_scores / total).astype(jnp.bfloat16))
    weights_wide = weights.astype(jnp.float32)
    attended = lax.optimization_barrier(jnp.einsum("cgqk,kcd->qcgd", weights_wide, v_bin).astype(jnp.bfloat16))
    row_delta = jnp.sum(d_bin * attended.astype(jnp.float32), axis=-1)
    dweights = jnp.einsum("qcgd,kcd->cgqk", d_bin, v_bin)
    dscores = lax.optimization_barrier(
        (weights_wide * (dweights - jnp.transpose(row_delta, (1, 2, 0))[..., None])).astype(jnp.bfloat16))
    dscores_wide = dscores.astype(jnp.float32)
    grad_q = (softmax_scale * jnp.einsum("cgqk,kcd->qcgd", dscores_wide, k_bin)).astype(jnp.bfloat16)
    grad_k = (softmax_scale * jnp.einsum("cgqk,qcgd->kcd", dscores_wide, q_bin)).astype(jnp.bfloat16)
    grad_v = jnp.einsum("cgqk,qcgd->kcd", weights_wide, d_bin).astype(jnp.bfloat16)
    return (grad_q.reshape(bin_span, HEADS * HEAD_DIM),
            grad_k.reshape(bin_span, KV_HEADS * HEAD_DIM),
            grad_v.reshape(bin_span, KV_HEADS * HEAD_DIM))


def reference(queries, key_rows, values, cotangent, block_route, doc_start):
    token_doc = jnp.repeat(doc_start, BLOCK)
    bins_total = TOKENS // (4 * BLOCK)

    def one_bin(bin_index):
        return bin_grads(queries, key_rows, values, cotangent, token_doc, bin_index)

    grad_q, grad_k, grad_v = lax.map(one_bin, jnp.arange(bins_total, dtype=jnp.int32))
    target = (block_route[:, 0] * BPD + block_route[:, 1]).astype(jnp.int32)

    def place(tensor):
        columns = tensor.shape[-1]
        blocks = tensor.reshape(BLOCKS, BLOCK, columns)
        return jnp.zeros_like(blocks).at[target].set(blocks).reshape(TOKENS, columns)

    return place(grad_q), place(grad_k), place(grad_v)
```

```python
import functools

import jax
import jax.numpy as jnp
import numpy as np
from jax import lax
from jax.experimental import pallas as pl
from jax.experimental.pallas import tpu as pltpu
from jax.sharding import PartitionSpec as P

HEAD_DIM = 128
BLOCK = 128
BIN = 4 * BLOCK
GROUP = 4
CHUNKS = 1 + GROUP
LANES = 2 * BLOCK
SCALE = HEAD_DIM ** -0.5
LOG2E = 1.4426950408889634
FAR = -1e30
MESH = pl.DeviceIdType.MESH
NT = (((1,), (1,)), ((), ()))


def dot(a, b, dims=(((1,), (0,)), ((), ()))):
    return lax.dot_general(a, b, dims, preferred_element_type=jnp.float32)


def fill_bias(bias, which, docs):
    row = lax.broadcasted_iota(jnp.int32, (BLOCK, BLOCK), 0)
    col = lax.broadcasted_iota(jnp.int32, (BLOCK, BLOCK), 1)
    causal = jnp.where(row <= col, 0.0, FAR)
    for half in range(2):
        for kb in range(2 * half + 2):
            for side in range(2):
                qb = 2 * half + side
                if kb == qb:
                    tile = causal
                elif kb > qb:
                    tile = jnp.full((BLOCK, BLOCK), FAR, jnp.float32)
                else:
                    tile = jnp.full((BLOCK, BLOCK), jnp.where(docs[kb] == docs[qb], 0.0, FAR), jnp.float32)
                bias[which, pl.ds(half * LANES + kb * BLOCK, BLOCK), pl.ds(side * BLOCK, BLOCK)] = tile


def head_grads(k, v, k_t, q, d, bias, which, grad_k, grad_v, first):
    parts = []
    for half in range(2):
        keys = (half + 1) * LANES
        rows = slice(half * LANES, (half + 1) * LANES)
        q_half, d_half = q[rows], d[rows]
        scores = dot(k[:keys], q_half, NT) * (SCALE * LOG2E) + bias[which, pl.ds(half * LANES, keys), :]
        scores = jnp.exp2(scores - jnp.max(scores, axis=0, keepdims=True))
        weights = scores * (1.0 / jnp.sum(scores, axis=0, keepdims=True))
        dweights = dot(v[:keys], d_half, NT)
        row_delta = jnp.sum(weights * dweights, axis=0, keepdims=True)
        dscores = (weights * (dweights - row_delta)).astype(jnp.bfloat16)
        add_v = dot(weights.astype(jnp.bfloat16), d_half)
        add_k = dot(dscores, q_half)
        if first and half == 0:
            grad_v[which, pl.ds(LANES, LANES), :] = jnp.zeros((LANES, HEAD_DIM), jnp.float32)
            grad_k[which, pl.ds(LANES, LANES), :] = jnp.zeros((LANES, HEAD_DIM), jnp.float32)
            grad_v[which, pl.ds(0, LANES), :] = add_v
            grad_k[which, pl.ds(0, LANES), :] = add_k
        else:
            grad_v[which, pl.ds(0, keys), :] += add_v
            grad_k[which, pl.ds(0, keys), :] += add_k
        parts.append(dot(k_t[:, :keys], dscores))
    return parts


def kernel(heads, bpd, *refs):
    sources, (route, doc), outs = refs[:4], refs[4:6], refs[6:9]
    xb, zs, zr = refs[9:14], refs[14:19], refs[19:24]
    k_t, bias, grad_k, grad_v, kept_q, route_s, doc_s = refs[24:31]
    x_send, x_recv, z_send, z_recv, own_sem, table_sem = refs[31:37]
    queries, key_rows, values, cotangent = sources
    me = lax.axis_index("head")
    dp = lax.axis_index("dp")
    mate = dp + 1 - 2 * (dp % 2)

    tables = [
        pltpu.make_async_copy(route, route_s, table_sem.at[0]),
        pltpu.make_async_copy(doc, doc_s, table_sem.at[1]),
    ]
    for copy in tables:
        copy.start()

    barrier = pltpu.get_barrier_semaphore()
    peers = [(me + step) % heads for step in range(1, heads)]
    for peer in peers:
        pl.semaphore_signal(barrier, inc=1, device_id=(dp, peer), device_id_type=MESH)
    pl.semaphore_signal(barrier, inc=1, device_id=(mate, me), device_id_type=MESH)

    def piece(chunk, which, peer):
        if chunk == 0:
            ref, first = (key_rows, values)[which], peer * HEAD_DIM
        else:
            ref, first = (queries, cotangent)[which], (peer * GROUP + chunk - 1) * HEAD_DIM
        return ref.at[:, pl.ds(pl.multiple_of(first, HEAD_DIM), HEAD_DIM)]

    def landing(chunk, which, block):
        return xb[chunk].at[which, block // 4, pl.ds(pl.multiple_of(block % 4 * BLOCK, BLOCK), BLOCK)]

    own = []
    for chunk in range(CHUNKS):
        for which in range(2):
            copy = pltpu.make_async_copy(
                piece(chunk, which, me), landing(chunk, which, me), own_sem.at[chunk, which]
            )
            copy.start()
            own.append(copy)
    pl.semaphore_wait(barrier, heads)

    sent = []
    for chunk in range(CHUNKS):
        for which in range(2):
            for step, peer in enumerate(peers):
                copy = pltpu.make_async_remote_copy(
                    src_ref=piece(chunk, which, peer),
                    dst_ref=landing(chunk, which, me),
                    send_sem=x_send.at[chunk, which, step],
                    recv_sem=x_recv.at[chunk, which, step],
                    device_id=(dp, peer),
                    device_id_type=MESH,
                )
                copy.start()
                sent.append(copy)

    for copy in tables:
        copy.wait()
    moved = jnp.where(route_s[0, dp * bpd] != dp, 0, 1)
    mate_moved = jnp.where(route_s[0, mate * bpd] != mate, 0, 1)
    kept = 1 - moved
    kept_docs = [doc_s[dp * bpd + kept * 4 + i] for i in range(4)]
    come_docs = [doc_s[mate * bpd + mate_moved * 4 + i] for i in range(4)]
    fill_bias(bias, 0, kept_docs)
    fill_bias(bias, 1, come_docs)

    def settle(stays, comes):
        return [jnp.where(moved == slot, comes, stays) for slot in range(2)]

    def keep(chunk):
        parts = head_grads(
            xb[0][0, kept], xb[0][1, kept], k_t[0], xb[chunk][0, kept], xb[chunk][1, kept],
            bias, 0, grad_k, grad_v, chunk == 1,
        )
        for half, part in enumerate(parts):
            kept_q[chunk - 1, pl.ds(half * LANES, LANES), :] = (part * SCALE).T

    def come(chunk):
        parts = head_grads(
            zr[0][0], zr[0][1], k_t[1], zr[chunk][0], zr[chunk][1],
            bias, 1, grad_k, grad_v, chunk == 1,
        )
        for half, part in enumerate(parts):
            stays = kept_q[chunk - 1, pl.ds(half * LANES, LANES), :]
            for slot, rows in enumerate(settle(stays, (part * SCALE).T)):
                outs[0][pl.ds(slot * BIN + half * LANES, LANES), pl.ds((chunk - 1) * HEAD_DIM, HEAD_DIM)] = (
                    rows.astype(jnp.bfloat16)
                )

    passed = []
    for chunk in range(CHUNKS):
        for copy in own[2 * chunk : 2 * chunk + 2]:
            copy.wait()
        for copy in sent[2 * (heads - 1) * chunk : 2 * (heads - 1) * (chunk + 1)]:
            copy.wait_recv()
        zs[chunk][...] = xb[chunk][:, moved]
        copy = pltpu.make_async_remote_copy(
            src_ref=zs[chunk],
            dst_ref=zr[chunk],
            send_sem=z_send.at[chunk],
            recv_sem=z_recv.at[chunk],
            device_id=(mate, me),
            device_id_type=MESH,
        )
        copy.start()
        passed.append(copy)
        if chunk == 0:
            k_t[0] = xb[0][0, kept].T
        else:
            keep(chunk)
            passed[chunk - 1].wait_recv()
            if chunk == 1:
                k_t[1] = zr[0][0].T
            else:
                come(chunk - 1)
    passed[-1].wait_recv()
    come(CHUNKS - 1)
    for out, total, scale in ((outs[1], grad_k, SCALE), (outs[2], grad_v, 1.0)):
        for slot, rows in enumerate(settle(total[0] * scale, total[1] * scale)):
            out[pl.ds(slot * BIN, BIN), :] = rows.astype(jnp.bfloat16)
    for copy in sent + passed:
        copy.wait_send()


def body(queries, key_rows, values, cotangent, block_route, doc_start):
    heads = lax.axis_size("head")
    bpd = block_route.shape[0] // lax.axis_size("dp")
    rows = bpd * BLOCK
    anywhere = pl.BlockSpec(memory_space=pl.ANY)
    vmem = pl.BlockSpec(memory_space=pltpu.VMEM)
    half, whole = (2, BIN, HEAD_DIM), (2, 2, BIN, HEAD_DIM)
    return pl.pallas_call(
        functools.partial(kernel, heads, bpd),
        out_shape=(
            jax.ShapeDtypeStruct((rows, GROUP * HEAD_DIM), jnp.bfloat16),
            jax.ShapeDtypeStruct((rows, HEAD_DIM), jnp.bfloat16),
            jax.ShapeDtypeStruct((rows, HEAD_DIM), jnp.bfloat16),
        ),
        in_specs=[anywhere] * 6,
        out_specs=[vmem] * 3,
        scratch_shapes=[pltpu.VMEM(whole, jnp.bfloat16)] * CHUNKS
        + [pltpu.VMEM(half, jnp.bfloat16)] * (2 * CHUNKS)
        + [
            pltpu.VMEM((2, HEAD_DIM, BIN), jnp.bfloat16),
            pltpu.VMEM((2, 3 * LANES, LANES), jnp.float32),
            pltpu.VMEM(half, jnp.float32),
            pltpu.VMEM(half, jnp.float32),
            pltpu.VMEM((GROUP, BIN, HEAD_DIM), jnp.float32),
            pltpu.SMEM((2, block_route.shape[0]), jnp.int32),
            pltpu.SMEM(doc_start.shape, jnp.int32),
            pltpu.SemaphoreType.DMA((CHUNKS, 2, heads - 1)),
            pltpu.SemaphoreType.DMA((CHUNKS, 2, heads - 1)),
            pltpu.SemaphoreType.DMA((CHUNKS,)),
            pltpu.SemaphoreType.DMA((CHUNKS,)),
            pltpu.SemaphoreType.DMA((CHUNKS, 2)),
            pltpu.SemaphoreType.DMA((2,)),
        ],
        compiler_params=pltpu.CompilerParams(
            collective_id=0, has_side_effects=True, vmem_limit_bytes=60 * 2**20
        ),
    )(queries, key_rows, values, cotangent, block_route.T, doc_start)


def solution(mesh):
    tokens = P(("dp", "head"), None)
    return jax.shard_map(
        body,
        mesh=mesh,
        in_specs=(tokens, tokens, tokens, tokens, P(), P()),
        out_specs=(P("dp", "head"), P("dp", "head"), P("dp", "head")),
        check_vma=False,
    )
```

```python
import functools

import jax
import jax.numpy as jnp
import numpy as np
from jax import lax
from jax.experimental import pallas as pl
from jax.experimental.pallas import tpu as pltpu
from jax.sharding import PartitionSpec as P

HEAD_DIM = 128
BLOCK = 128
BIN = 4 * BLOCK
GROUP = 4
CHUNKS = 1 + GROUP
LANES = 2 * BLOCK
ARRAYS = 2 * CHUNKS
SCALE = HEAD_DIM ** -0.5
LOG2E = 1.4426950408889634
FAR = -1e30
MESH = pl.DeviceIdType.MESH
NT = (((1,), (1,)), ((), ()))


def dot(a, b, dims=(((1,), (0,)), ((), ()))):
    return lax.dot_general(a, b, dims, preferred_element_type=jnp.float32)


def fill_bias(bias, which, docs):
    row = lax.broadcasted_iota(jnp.int32, (BLOCK, BLOCK), 0)
    col = lax.broadcasted_iota(jnp.int32, (BLOCK, BLOCK), 1)
    causal = jnp.where(row <= col, 0.0, FAR)
    for half in range(2):
        for kb in range(2 * half + 2):
            for side in range(2):
                qb = 2 * half + side
                if kb == qb:
                    tile = causal
                elif kb > qb:
                    tile = jnp.full((BLOCK, BLOCK), FAR, jnp.float32)
                else:
                    tile = jnp.full((BLOCK, BLOCK), jnp.where(docs[kb] == docs[qb], 0.0, FAR), jnp.float32)
                bias[which, pl.ds(half * LANES + kb * BLOCK, BLOCK), pl.ds(side * BLOCK, BLOCK)] = tile


def halves():
    for half in range(2):
        yield pl.ds(half * LANES, LANES), half * LANES, (half + 1) * LANES


def weigh(k, q, bias, weights):
    for _, first, keys in halves():
        scores = dot(k[:keys], q[first : first + LANES], NT) * (SCALE * LOG2E) + bias[pl.ds(first, keys), :]
        scores = jnp.exp2(scores - jnp.max(scores, axis=0, keepdims=True))
        weights[pl.ds(first, keys), :] = scores * (1.0 / jnp.sum(scores, axis=0, keepdims=True))


def spread(v, k_t, q, d, weights, grad_k, grad_v, opens):
    parts = []
    for rows, first, keys in halves():
        q_half, d_half = q[first : first + LANES], d[first : first + LANES]
        share = weights[pl.ds(first, keys), :]
        dweights = dot(v[:keys], d_half, NT)
        row_delta = jnp.sum(share * dweights, axis=0, keepdims=True)
        dscores = (share * (dweights - row_delta)).astype(jnp.bfloat16)
        add_v = dot(share.astype(jnp.bfloat16), d_half)
        add_k = dot(dscores, q_half)
        if opens and first == 0:
            later = pl.ds(LANES, LANES)
            for total, add in ((grad_v, add_v), (grad_k, add_k)):
                total[later, :] = jnp.zeros((LANES, HEAD_DIM), jnp.float32)
                total[pl.ds(0, LANES), :] = add
        else:
            grad_v[pl.ds(0, keys), :] += add_v
            grad_k[pl.ds(0, keys), :] += add_k
        parts.append((rows, first, (dot(k_t[:, :keys], dscores) * SCALE).T))
    return parts


def kernel(heads, bpd, *refs):
    (queries, key_rows, values, cotangent), (route, doc), (out_q, out_k, out_v) = refs[:4], refs[4:6], refs[6:9]
    xb, zs, zr = (refs[9 + n * ARRAYS : 9 + (n + 1) * ARRAYS] for n in range(3))
    k_t, bias, weights, grad_k, grad_v, kept_q, route_s, doc_s = refs[39:47]
    x_send, x_recv, z_send, z_recv, own_sem, table_sem = refs[47:53]
    me = lax.axis_index("head")
    dp = lax.axis_index("dp")
    mate = dp + 1 - 2 * (dp % 2)
    peers = [(me + step) % heads for step in range(1, heads)]

    barrier = pltpu.get_barrier_semaphore()
    for peer in peers:
        pl.semaphore_signal(barrier, inc=1, device_id=(dp, peer), device_id_type=MESH)
    pl.semaphore_signal(barrier, inc=1, device_id=(mate, me), device_id_type=MESH)

    tables = [
        pltpu.make_async_copy(route, route_s, table_sem.at[0]),
        pltpu.make_async_copy(doc, doc_s, table_sem.at[1]),
    ]
    for copy in tables:
        copy.start()

    def source(n, peer):
        if n < 2:
            ref, first = (key_rows, values)[n], peer * HEAD_DIM
        else:
            ref, first = (queries, cotangent)[n % 2], (peer * GROUP + n // 2 - 1) * HEAD_DIM
        return ref.at[:, pl.ds(pl.multiple_of(first, HEAD_DIM), HEAD_DIM)]

    def landing(n):
        return xb[n].at[me // 4, pl.ds(pl.multiple_of(me % 4 * BLOCK, BLOCK), BLOCK)]

    own, sent = [], []
    for n in range(ARRAYS):
        copy = pltpu.make_async_copy(source(n, me), landing(n), own_sem.at[n])
        copy.start()
        own.append(copy)
    pl.semaphore_wait(barrier, heads)
    for n in range(ARRAYS):
        sent.append([])
        for step, peer in enumerate(peers):
            copy = pltpu.make_async_remote_copy(
                src_ref=source(n, peer),
                dst_ref=landing(n),
                send_sem=x_send.at[n, step],
                recv_sem=x_recv.at[n, step],
                device_id=(dp, peer),
                device_id_type=MESH,
            )
            copy.start()
            sent[-1].append(copy)

    for copy in tables:
        copy.wait()
    moved = jnp.where(route_s[0, dp * bpd] != dp, 0, 1)
    mate_moved = jnp.where(route_s[0, mate * bpd] != mate, 0, 1)
    kept = 1 - moved
    fill_bias(bias, 0, [doc_s[dp * bpd + kept * 4 + i] for i in range(4)])
    fill_bias(bias, 1, [doc_s[mate * bpd + mate_moved * 4 + i] for i in range(4)])

    def settle(stays, comes):
        return [jnp.where(moved == slot, comes, stays) for slot in range(2)]

    def work(side, n):
        def bin_of(n):
            return zr[n][...] if side else xb[n][kept]

        if n == 0:
            k_t[side] = bin_of(0).T
        elif n > 1 and n % 2 == 0:
            weigh(bin_of(0), bin_of(n), bias.at[side], weights.at[side])
        elif n > 1:
            parts = spread(
                bin_of(1), k_t[side], bin_of(n - 1), bin_of(n), weights.at[side],
                grad_k.at[side], grad_v.at[side], n == 3,
            )
            head = n // 2 - 1
            for rows, first, part in parts:
                if side == 0:
                    kept_q[head, rows, :] = part
                    continue
                for slot, settled in enumerate(settle(kept_q[head, rows, :], part)):
                    out_q[pl.ds(slot * BIN + first, LANES), pl.ds(head * HEAD_DIM, HEAD_DIM)] = settled.astype(
                        jnp.bfloat16
                    )

    passed = []
    for n in range(ARRAYS):
        own[n].wait()
        for copy in sent[n]:
            copy.wait_recv()
        zs[n][...] = xb[n][moved]
        copy = pltpu.make_async_remote_copy(
            src_ref=zs[n],
            dst_ref=zr[n],
            send_sem=z_send.at[n],
            recv_sem=z_recv.at[n],
            device_id=(mate, me),
            device_id_type=MESH,
        )
        copy.start()
        passed.append(copy)
        work(0, n)
        if n > 0:
            passed[n - 1].wait_recv()
            work(1, n - 1)
    passed[-1].wait_recv()
    work(1, ARRAYS - 1)
    for out, total, scale in ((out_k, grad_k, SCALE), (out_v, grad_v, 1.0)):
        for slot, settled in enumerate(settle(total[0] * scale, total[1] * scale)):
            out[pl.ds(slot * BIN, BIN), :] = settled.astype(jnp.bfloat16)
    for copy in [copy for group in sent for copy in group] + passed:
        copy.wait_send()


def write(*refs):
    copies = [pltpu.make_async_copy(refs[n], refs[n + 3], refs[6].at[n]) for n in range(3)]
    for copy in copies:
        copy.start()
    for copy in copies:
        copy.wait()


def body(queries, key_rows, values, cotangent, block_route, doc_start):
    heads = lax.axis_size("head")
    bpd = block_route.shape[0] // lax.axis_size("dp")
    rows = bpd * BLOCK
    anywhere = pl.BlockSpec(memory_space=pl.ANY)
    vmem = pl.BlockSpec(memory_space=pltpu.VMEM)
    shapes = [(rows, GROUP * HEAD_DIM), (rows, HEAD_DIM), (rows, HEAD_DIM)]
    arguments = [
        pltpu.with_memory_space_constraint(x, pltpu.HBM)
        for x in (queries, key_rows, values, cotangent, block_route.T, doc_start)
    ]
    held = pl.pallas_call(
        functools.partial(kernel, heads, bpd),
        out_shape=[pltpu.VMEM(shape, jnp.bfloat16) for shape in shapes],
        in_specs=[anywhere] * 6,
        out_specs=[vmem] * 3,
        scratch_shapes=[pltpu.VMEM((2, BIN, HEAD_DIM), jnp.bfloat16)] * ARRAYS
        + [pltpu.VMEM((BIN, HEAD_DIM), jnp.bfloat16)] * (2 * ARRAYS)
        + [
            pltpu.VMEM((2, HEAD_DIM, BIN), jnp.bfloat16),
            pltpu.VMEM((2, 3 * LANES, LANES), jnp.float32),
            pltpu.VMEM((2, 3 * LANES, LANES), jnp.float32),
            pltpu.VMEM((2, BIN, HEAD_DIM), jnp.float32),
            pltpu.VMEM((2, BIN, HEAD_DIM), jnp.float32),
            pltpu.VMEM((GROUP, BIN, HEAD_DIM), jnp.float32),
            pltpu.SMEM((2, block_route.shape[0]), jnp.int32),
            pltpu.SMEM(doc_start.shape, jnp.int32),
            pltpu.SemaphoreType.DMA((ARRAYS, heads - 1)),
            pltpu.SemaphoreType.DMA((ARRAYS, heads - 1)),
            pltpu.SemaphoreType.DMA((ARRAYS,)),
            pltpu.SemaphoreType.DMA((ARRAYS,)),
            pltpu.SemaphoreType.DMA((ARRAYS,)),
            pltpu.SemaphoreType.DMA((2,)),
        ],
        compiler_params=pltpu.CompilerParams(
            collective_id=0, has_side_effects=True, vmem_limit_bytes=40 * 2**20
        ),
    )(*arguments)
    return pl.pallas_call(
        write,
        out_shape=[jax.ShapeDtypeStruct(shape, jnp.bfloat16) for shape in shapes],
        in_specs=[vmem] * 3,
        out_specs=[anywhere] * 3,
        scratch_shapes=[pltpu.SemaphoreType.DMA((3,))],
        compiler_params=pltpu.CompilerParams(vmem_limit_bytes=2**20),
    )(*(pltpu.with_memory_space_constraint(x, pltpu.VMEM) for x in held))


def solution(mesh):
    tokens = P(("dp", "head"), None)
    return jax.shard_map(
        body,
        mesh=mesh,
        in_specs=(tokens, tokens, tokens, tokens, P(), P()),
        out_specs=(P("dp", "head"), P("dp", "head"), P("dp", "head")),
        check_vma=False,
    )
```

```python
import functools

import jax
import jax.numpy as jnp
import numpy as np
from jax import lax
from jax.experimental import pallas as pl
from jax.experimental.pallas import tpu as pltpu
from jax.sharding import PartitionSpec as P

HEAD_DIM = 128
BLOCK = 128
BIN = 4 * BLOCK
GROUP = 4
CHUNKS = 1 + GROUP
LANES = 2 * BLOCK
ARRAYS = 2 * CHUNKS
SCALE = HEAD_DIM ** -0.5
LOG2E = 1.4426950408889634
FAR = -1e30
MESH = pl.DeviceIdType.MESH
NT = (((1,), (1,)), ((), ()))


def dot(a, b, dims=(((1,), (0,)), ((), ()))):
    return lax.dot_general(a, b, dims, preferred_element_type=jnp.float32)


def fill_bias(bias, which, docs):
    row = lax.broadcasted_iota(jnp.int32, (BLOCK, BLOCK), 0)
    col = lax.broadcasted_iota(jnp.int32, (BLOCK, BLOCK), 1)
    causal = jnp.where(row <= col, 0.0, FAR)
    for half in range(2):
        for kb in range(2 * half + 2):
            for side in range(2):
                qb = 2 * half + side
                if kb == qb:
                    tile = causal
                elif kb > qb:
                    tile = jnp.full((BLOCK, BLOCK), FAR, jnp.float32)
                else:
                    tile = jnp.full((BLOCK, BLOCK), jnp.where(docs[kb] == docs[qb], 0.0, FAR), jnp.float32)
                bias[which, pl.ds(half * LANES + kb * BLOCK, BLOCK), pl.ds(side * BLOCK, BLOCK)] = tile


def weigh(k, q, bias, weights):
    for half in range(2):
        first, keys = half * LANES, (half + 1) * LANES
        scores = dot(k[:keys], q[first : first + LANES], NT) * (SCALE * LOG2E) + bias[pl.ds(first, keys), :]
        scores = jnp.exp2(scores - jnp.max(scores, axis=0, keepdims=True))
        weights[pl.ds(first, keys), :] = scores * (1.0 / jnp.sum(scores, axis=0, keepdims=True))


def spread(half, v, k_t, q, d, weights, grad_k, grad_v, opens):
    keys = (half + 1) * LANES
    share = weights[pl.ds(half * LANES, keys), :]
    dweights = dot(v[:keys], d, NT)
    row_delta = jnp.sum(share * dweights, axis=0, keepdims=True)
    dscores = (share * (dweights - row_delta)).astype(jnp.bfloat16)
    for total, add in ((grad_v, dot(share.astype(jnp.bfloat16), d)), (grad_k, dot(dscores, q))):
        if opens and half == 1:
            total[...] = add
        else:
            total[pl.ds(0, keys), :] += add
    return (dot(k_t[:, :keys], dscores) * SCALE).T


def kernel(heads, bpd, *refs):
    (queries, key_rows, values, cotangent), (route, doc), (out_q, out_k, out_v) = refs[:4], refs[4:6], refs[6:9]
    xb, zs, zr = (refs[9 + n * ARRAYS : 9 + (n + 1) * ARRAYS] for n in range(3))
    k_t, bias, weights, grad_k, grad_v, kept_q, route_s, doc_s = refs[39:47]
    x_send, x_recv, z_send, z_recv, own_sem, table_sem = refs[47:53]
    me = lax.axis_index("head")
    dp = lax.axis_index("dp")
    mate = dp + 1 - 2 * (dp % 2)
    peers = [(me + step) % heads for step in range(1, heads)]

    barrier = pltpu.get_barrier_semaphore()
    for peer in peers:
        pl.semaphore_signal(barrier, inc=1, device_id=(dp, peer), device_id_type=MESH)
    pl.semaphore_signal(barrier, inc=1, device_id=(mate, me), device_id_type=MESH)

    tables = [
        pltpu.make_async_copy(route, route_s, table_sem.at[0]),
        pltpu.make_async_copy(doc, doc_s, table_sem.at[1]),
    ]
    for copy in tables:
        copy.start()

    def source(n, peer):
        if n < 2:
            ref, first = (key_rows, values)[n], peer * HEAD_DIM
        else:
            ref, first = (queries, cotangent)[n % 2], (peer * GROUP + n // 2 - 1) * HEAD_DIM
        return ref.at[:, pl.ds(pl.multiple_of(first, HEAD_DIM), HEAD_DIM)]

    def landing(n):
        return xb[n].at[me // 4, pl.ds(pl.multiple_of(me % 4 * BLOCK, BLOCK), BLOCK)]

    own, sent = [], []
    for n in range(ARRAYS):
        copy = pltpu.make_async_copy(source(n, me), landing(n), own_sem.at[n])
        copy.start()
        own.append(copy)
    pl.semaphore_wait(barrier, heads)
    for n in range(ARRAYS):
        sent.append([])
        for step, peer in enumerate(peers):
            copy = pltpu.make_async_remote_copy(
                src_ref=source(n, peer),
                dst_ref=landing(n),
                send_sem=x_send.at[n, step],
                recv_sem=x_recv.at[n, step],
                device_id=(dp, peer),
                device_id_type=MESH,
            )
            copy.start()
            sent[-1].append(copy)

    for copy in tables:
        copy.wait()
    moved = jnp.where(route_s[0, dp * bpd] != dp, 0, 1)
    mate_moved = jnp.where(route_s[0, mate * bpd] != mate, 0, 1)
    kept = 1 - moved
    fill_bias(bias, 0, [doc_s[dp * bpd + kept * 4 + i] for i in range(4)])
    fill_bias(bias, 1, [doc_s[mate * bpd + mate_moved * 4 + i] for i in range(4)])

    def settle(stays, comes):
        return [jnp.where(moved == slot, comes, stays) for slot in range(2)]

    def work(side, n, half):
        rows = pl.ds(half * LANES, LANES)

        def bin_of(n):
            return zr[n][...] if side else xb[n][kept]

        def half_of(n):
            return zr[n][rows, :] if side else xb[n][kept, rows, :]

        if n == 0 and half == 0:
            k_t[side] = bin_of(0).T
        elif n > 1 and n % 2 == 0 and half == 0:
            weigh(bin_of(0), bin_of(n), bias.at[side], weights.at[side])
        elif n > 1 and n % 2:
            part = spread(
                half, bin_of(1), k_t[side], half_of(n - 1), half_of(n), weights.at[side],
                grad_k.at[side], grad_v.at[side], n == 3,
            )
            head = n // 2 - 1
            if side == 0:
                kept_q[head, rows, :] = part
                return
            for slot, settled in enumerate(settle(kept_q[head, rows, :], part)):
                out_q[pl.ds(slot * BIN + half * LANES, LANES), pl.ds(head * HEAD_DIM, HEAD_DIM)] = settled.astype(
                    jnp.bfloat16
                )

    def forward(n, half):
        rows = pl.ds(0, BIN) if half is None else pl.ds(half * LANES, LANES)
        copy = pltpu.make_async_remote_copy(
            src_ref=zs[n].at[rows],
            dst_ref=zr[n].at[rows],
            send_sem=z_send.at[n, half or 0],
            recv_sem=z_recv.at[n, half or 0],
            device_id=(mate, me),
            device_id_type=MESH,
        )
        copy.start()
        return copy

    last, passed = ARRAYS - 1, []
    for n in range(ARRAYS):
        own[n].wait()
        for copy in sent[n]:
            copy.wait_recv()
        zs[n][...] = xb[n][moved]
        passed.append([forward(n, half) for half in ((1, 0) if n == last else (None,))])
        for half in (1, 0):
            work(0, n, half)
        if n > 0:
            passed[n - 1][0].wait_recv()
            for half in (1, 0):
                work(1, n - 1, half)
    for half, copy in zip((1, 0), passed[last]):
        copy.wait_recv()
        work(1, last, half)
        rows = pl.ds(half * LANES, LANES)
        for out, total, scale in ((out_k, grad_k, SCALE), (out_v, grad_v, 1.0)):
            for slot, settled in enumerate(settle(total[0, rows, :] * scale, total[1, rows, :] * scale)):
                out[pl.ds(slot * BIN + half * LANES, LANES), :] = settled.astype(jnp.bfloat16)
    for copy in [copy for group in sent + passed for copy in group]:
        copy.wait_send()


def write(*refs):
    copies = [pltpu.make_async_copy(refs[n], refs[n + 3], refs[6].at[n]) for n in range(3)]
    for copy in copies:
        copy.start()
    for copy in copies:
        copy.wait()


def body(queries, key_rows, values, cotangent, block_route, doc_start):
    heads = lax.axis_size("head")
    bpd = block_route.shape[0] // lax.axis_size("dp")
    rows = bpd * BLOCK
    anywhere = pl.BlockSpec(memory_space=pl.ANY)
    vmem = pl.BlockSpec(memory_space=pltpu.VMEM)
    shapes = [(rows, GROUP * HEAD_DIM), (rows, HEAD_DIM), (rows, HEAD_DIM)]
    arguments = [
        pltpu.with_memory_space_constraint(x, pltpu.HBM)
        for x in (queries, key_rows, values, cotangent, block_route.T, doc_start)
    ]
    held = pl.pallas_call(
        functools.partial(kernel, heads, bpd),
        out_shape=[pltpu.VMEM(shape, jnp.bfloat16) for shape in shapes],
        in_specs=[anywhere] * 6,
        out_specs=[vmem] * 3,
        scratch_shapes=[pltpu.VMEM((2, BIN, HEAD_DIM), jnp.bfloat16)] * ARRAYS
        + [pltpu.VMEM((BIN, HEAD_DIM), jnp.bfloat16)] * (2 * ARRAYS)
        + [
            pltpu.VMEM((2, HEAD_DIM, BIN), jnp.bfloat16),
            pltpu.VMEM((2, 3 * LANES, LANES), jnp.float32),
            pltpu.VMEM((2, 3 * LANES, LANES), jnp.float32),
            pltpu.VMEM((2, BIN, HEAD_DIM), jnp.float32),
            pltpu.VMEM((2, BIN, HEAD_DIM), jnp.float32),
            pltpu.VMEM((GROUP, BIN, HEAD_DIM), jnp.float32),
            pltpu.SMEM((2, block_route.shape[0]), jnp.int32),
            pltpu.SMEM(doc_start.shape, jnp.int32),
            pltpu.SemaphoreType.DMA((ARRAYS, heads - 1)),
            pltpu.SemaphoreType.DMA((ARRAYS, heads - 1)),
            pltpu.SemaphoreType.DMA((ARRAYS, 2)),
            pltpu.SemaphoreType.DMA((ARRAYS, 2)),
            pltpu.SemaphoreType.DMA((ARRAYS,)),
            pltpu.SemaphoreType.DMA((2,)),
        ],
        compiler_params=pltpu.CompilerParams(
            collective_id=0, has_side_effects=True, vmem_limit_bytes=40 * 2**20
        ),
    )(*arguments)
    return pl.pallas_call(
        write,
        out_shape=[jax.ShapeDtypeStruct(shape, jnp.bfloat16) for shape in shapes],
        in_specs=[vmem] * 3,
        out_specs=[anywhere] * 3,
        scratch_shapes=[pltpu.SemaphoreType.DMA((3,))],
        compiler_params=pltpu.CompilerParams(vmem_limit_bytes=2**20),
    )(*(pltpu.with_memory_space_constraint(x, pltpu.VMEM) for x in held))


def solution(mesh):
    tokens = P(("dp", "head"), None)
    return jax.shard_map(
        body,
        mesh=mesh,
        in_specs=(tokens, tokens, tokens, tokens, P(), P()),
        out_specs=(P("dp", "head"), P("dp", "head"), P("dp", "head")),
        check_vma=False,
    )
```

```python
import functools

import jax
import jax.numpy as jnp
import numpy as np
from jax import lax
from jax.experimental import pallas as pl
from jax.experimental.pallas import tpu as pltpu
from jax.sharding import PartitionSpec as P

HEAD_DIM = 128
BLOCK = 128
BIN = 4 * BLOCK
GROUP = 4
CHUNKS = 1 + GROUP
LANES = 2 * BLOCK
ARRAYS = 2 * CHUNKS
SCALE = HEAD_DIM ** -0.5
LOG2E = 1.4426950408889634
FAR = -1e30
MESH = pl.DeviceIdType.MESH
NT = (((1,), (1,)), ((), ()))


def dot(a, b, dims=(((1,), (0,)), ((), ()))):
    return lax.dot_general(a, b, dims, preferred_element_type=jnp.float32)


def fill_bias(bias, which, docs):
    row = lax.broadcasted_iota(jnp.int32, (BLOCK, BLOCK), 0)
    col = lax.broadcasted_iota(jnp.int32, (BLOCK, BLOCK), 1)
    causal = jnp.where(row <= col, 0.0, FAR)
    for half in range(2):
        for kb in range(2 * half + 2):
            for side in range(2):
                qb = 2 * half + side
                if kb == qb:
                    tile = causal
                elif kb > qb:
                    tile = jnp.full((BLOCK, BLOCK), FAR, jnp.float32)
                else:
                    tile = jnp.full((BLOCK, BLOCK), jnp.where(docs[kb] == docs[qb], 0.0, FAR), jnp.float32)
                bias[which, pl.ds(half * LANES + kb * BLOCK, BLOCK), pl.ds(side * BLOCK, BLOCK)] = tile


def weigh(k, q, bias, weights):
    for half in range(2):
        first, keys = half * LANES, (half + 1) * LANES
        scores = dot(k[:keys], q[first : first + LANES], NT) * (SCALE * LOG2E) + bias[pl.ds(first, keys), :]
        scores = jnp.exp2(scores - jnp.max(scores, axis=0, keepdims=True))
        weights[pl.ds(first, keys), :] = scores * (1.0 / jnp.sum(scores, axis=0, keepdims=True))


def spread(half, v, k_t, q, d, weights, grad_k, grad_v, opens):
    keys = (half + 1) * LANES
    share = weights[pl.ds(half * LANES, keys), :]
    dweights = dot(v[:keys], d, NT)
    row_delta = jnp.sum(share * dweights, axis=0, keepdims=True)
    dscores = (share * (dweights - row_delta)).astype(jnp.bfloat16)
    for total, add in ((grad_v, dot(share.astype(jnp.bfloat16), d)), (grad_k, dot(dscores, q))):
        if opens and half == 1:
            total[...] = add
        else:
            total[pl.ds(0, keys), :] += add
    return (dot(k_t[:, :keys], dscores) * SCALE).T


def kernel(heads, bpd, *refs):
    (queries, key_rows, values, cotangent), (route, doc), (out_q, out_k, out_v) = refs[:4], refs[4:6], refs[6:9]
    xb, zs, zr = (refs[9 + n * ARRAYS : 9 + (n + 1) * ARRAYS] for n in range(3))
    k_t, bias, weights, grad_k, grad_v, kept_q, route_s, doc_s = refs[39:47]
    x_send, x_recv, z_send, z_recv, own_sem, table_sem = refs[47:53]
    me = lax.axis_index("head")
    dp = lax.axis_index("dp")
    mate = dp + 1 - 2 * (dp % 2)
    peers = [(me + step) % heads for step in range(1, heads)]

    barrier = pltpu.get_barrier_semaphore()
    for peer in peers:
        pl.semaphore_signal(barrier, inc=1, device_id=(dp, peer), device_id_type=MESH)
    pl.semaphore_signal(barrier, inc=1, device_id=(mate, me), device_id_type=MESH)

    tables = [
        pltpu.make_async_copy(route, route_s, table_sem.at[0]),
        pltpu.make_async_copy(doc, doc_s, table_sem.at[1]),
    ]
    def source(n, peer):
        if n < 2:
            ref, first = (key_rows, values)[n], peer * HEAD_DIM
        else:
            ref, first = (queries, cotangent)[n % 2], (peer * GROUP + n // 2 - 1) * HEAD_DIM
        return ref.at[:, pl.ds(pl.multiple_of(first, HEAD_DIM), HEAD_DIM)]

    def landing(n):
        return xb[n].at[me // 4, pl.ds(pl.multiple_of(me % 4 * BLOCK, BLOCK), BLOCK)]

    own, sent = [], []
    pl.semaphore_wait(barrier, heads)
    for n in range(ARRAYS):
        sent.append([])
        for step, peer in enumerate(peers):
            copy = pltpu.make_async_remote_copy(
                src_ref=source(n, peer),
                dst_ref=landing(n),
                send_sem=x_send.at[n, step],
                recv_sem=x_recv.at[n, step],
                device_id=(dp, peer),
                device_id_type=MESH,
            )
            copy.start()
            sent[-1].append(copy)
        copy = pltpu.make_async_copy(source(n, me), landing(n), own_sem.at[n])
        copy.start()
        own.append(copy)
        if n == 0:
            for copy in tables:
                copy.start()

    for copy in tables:
        copy.wait()
    moved = jnp.where(route_s[0, dp * bpd] != dp, 0, 1)
    mate_moved = jnp.where(route_s[0, mate * bpd] != mate, 0, 1)
    kept = 1 - moved
    fill_bias(bias, 0, [doc_s[dp * bpd + kept * 4 + i] for i in range(4)])
    fill_bias(bias, 1, [doc_s[mate * bpd + mate_moved * 4 + i] for i in range(4)])

    def settle(stays, comes):
        return [jnp.where(moved == slot, comes, stays) for slot in range(2)]

    def work(side, n, half):
        rows = pl.ds(half * LANES, LANES)

        def bin_of(n):
            return zr[n][...] if side else xb[n][kept]

        def half_of(n):
            return zr[n][rows, :] if side else xb[n][kept, rows, :]

        if n == 0 and half == 0:
            k_t[side] = bin_of(0).T
        elif n > 1 and n % 2 == 0 and half == 0:
            weigh(bin_of(0), bin_of(n), bias.at[side], weights.at[side])
        elif n > 1 and n % 2:
            part = spread(
                half, bin_of(1), k_t[side], half_of(n - 1), half_of(n), weights.at[side],
                grad_k.at[side], grad_v.at[side], n == 3,
            )
            head = n // 2 - 1
            if side == 0:
                kept_q[head, rows, :] = part
                return
            for slot, settled in enumerate(settle(kept_q[head, rows, :], part)):
                out_q[pl.ds(slot * BIN + half * LANES, LANES), pl.ds(head * HEAD_DIM, HEAD_DIM)] = settled.astype(
                    jnp.bfloat16
                )

    def forward(n, half):
        rows = pl.ds(0, BIN) if half is None else pl.ds(half * LANES, LANES)
        copy = pltpu.make_async_remote_copy(
            src_ref=zs[n].at[rows],
            dst_ref=zr[n].at[rows],
            send_sem=z_send.at[n, half or 0],
            recv_sem=z_recv.at[n, half or 0],
            device_id=(mate, me),
            device_id_type=MESH,
        )
        copy.start()
        return copy

    last, passed = ARRAYS - 1, []
    for n in range(ARRAYS):
        own[n].wait()
        for copy in sent[n]:
            copy.wait_recv()
        zs[n][...] = xb[n][moved]
        passed.append([forward(n, half) for half in ((1, 0) if n == last else (None,))])
        for half in (1, 0):
            work(0, n, half)
        if n > 0:
            passed[n - 1][0].wait_recv()
            for half in (1, 0):
                work(1, n - 1, half)
    for half, copy in zip((1, 0), passed[last]):
        copy.wait_recv()
        work(1, last, half)
        rows = pl.ds(half * LANES, LANES)
        for out, total, scale in ((out_k, grad_k, SCALE), (out_v, grad_v, 1.0)):
            for slot, settled in enumerate(settle(total[0, rows, :] * scale, total[1, rows, :] * scale)):
                out[pl.ds(slot * BIN + half * LANES, LANES), :] = settled.astype(jnp.bfloat16)
    for copy in [copy for group in sent + passed for copy in group]:
        copy.wait_send()


def write(*refs):
    copies = [pltpu.make_async_copy(refs[n], refs[n + 3], refs[6].at[n]) for n in range(3)]
    for copy in copies:
        copy.start()
    for copy in copies:
        copy.wait()


def body(queries, key_rows, values, cotangent, block_route, doc_start):
    heads = lax.axis_size("head")
    bpd = block_route.shape[0] // lax.axis_size("dp")
    rows = bpd * BLOCK
    anywhere = pl.BlockSpec(memory_space=pl.ANY)
    vmem = pl.BlockSpec(memory_space=pltpu.VMEM)
    shapes = [(rows, GROUP * HEAD_DIM), (rows, HEAD_DIM), (rows, HEAD_DIM)]
    arguments = [
        pltpu.with_memory_space_constraint(x, pltpu.HBM)
        for x in (queries, key_rows, values, cotangent, block_route.T, doc_start)
    ]
    held = pl.pallas_call(
        functools.partial(kernel, heads, bpd),
        out_shape=[pltpu.VMEM(shape, jnp.bfloat16) for shape in shapes],
        in_specs=[anywhere] * 6,
        out_specs=[vmem] * 3,
        scratch_shapes=[pltpu.VMEM((2, BIN, HEAD_DIM), jnp.bfloat16)] * ARRAYS
        + [pltpu.VMEM((BIN, HEAD_DIM), jnp.bfloat16)] * (2 * ARRAYS)
        + [
            pltpu.VMEM((2, HEAD_DIM, BIN), jnp.bfloat16),
            pltpu.VMEM((2, 3 * LANES, LANES), jnp.float32),
            pltpu.VMEM((2, 3 * LANES, LANES), jnp.float32),
            pltpu.VMEM((2, BIN, HEAD_DIM), jnp.float32),
            pltpu.VMEM((2, BIN, HEAD_DIM), jnp.float32),
            pltpu.VMEM((GROUP, BIN, HEAD_DIM), jnp.float32),
            pltpu.SMEM((2, block_route.shape[0]), jnp.int32),
            pltpu.SMEM(doc_start.shape, jnp.int32),
            pltpu.SemaphoreType.DMA((ARRAYS, heads - 1)),
            pltpu.SemaphoreType.DMA((ARRAYS, heads - 1)),
            pltpu.SemaphoreType.DMA((ARRAYS, 2)),
            pltpu.SemaphoreType.DMA((ARRAYS, 2)),
            pltpu.SemaphoreType.DMA((ARRAYS,)),
            pltpu.SemaphoreType.DMA((2,)),
        ],
        compiler_params=pltpu.CompilerParams(
            collective_id=0, has_side_effects=True, vmem_limit_bytes=40 * 2**20
        ),
    )(*arguments)
    return pl.pallas_call(
        write,
        out_shape=[jax.ShapeDtypeStruct(shape, jnp.bfloat16) for shape in shapes],
        in_specs=[vmem] * 3,
        out_specs=[anywhere] * 3,
        scratch_shapes=[pltpu.SemaphoreType.DMA((3,))],
        compiler_params=pltpu.CompilerParams(vmem_limit_bytes=2**20),
    )(*(pltpu.with_memory_space_constraint(x, pltpu.VMEM) for x in held))


def solution(mesh):
    tokens = P(("dp", "head"), None)
    return jax.shard_map(
        body,
        mesh=mesh,
        in_specs=(tokens, tokens, tokens, tokens, P(), P()),
        out_specs=(P("dp", "head"), P("dp", "head"), P("dp", "head")),
        check_vma=False,
    )
```
